512 devices in a mesh: row: 32 (over y, x_lo, core), col: 16 (over z, x_hi).
Axes of the slice: x: 4 (x_hi: 2, x_lo: 2; x = x_hi * 2 + x_lo), y: 8, z: 8, core: 2. Of those that a mesh axis runs over, the one named last changes fastest.
Arguments:
- vectors: bfloat16 [64, 65536], P(None, ('row', 'col')), may hold values from -6 to 6
- tiles: bfloat16 [32, 16, 20, 128, 128], P('row', 'col'), may hold values from -0.078125 to 0.078125
- tile_row: int32 [32, 16, 20], P('row', 'col'), may hold values from -1 to 15, as said below
- tile_col: int32 [32, 16, 20], P('row', 'col'), may hold values from -1 to 31, as said below
Outputs:
- first_degree: bfloat16 [64, 65536], P(None, ('row', 'col'))
- second_degree: float32 [64, 65536], P(None, ('row', 'col'))
The draws below stay inside these ranges and needn't reach their ends.
Inputs may be any that keep to these rules, and one draw needn't show every extreme that they name: tile_row and tile_col are -1 in the same slots. Slots of a device form groups of 16 in order (slot s in group floor(s / 16)); the slots of the first group are never empty. Within a group, the live slots have distinct values of tile_row. `tile_col`: see tile_row.
All inputs are finite; a program needn't handle non-finite values.
Results may differ from the reference program's by a relative error of at most 0.0025.
Values may be sent and summed in bfloat16 or wider, within the bound.
A program may use at most 64 MiB of HBM per device.

```python
import jax
import jax.numpy as jnp
from jax import lax

B = 128
V = 64
BPD = 1
TILES_ROW = 20
KMAX = 20
NB = 512
N = 65536
N_ROW = 32
N_COL = 16


def shared_pattern(key):
    key_perm, key_rem_row, key_rem_col, key_live, key_offset = jax.random.split(key, 5)
    depth = (KMAX + N_COL - 1) // N_COL
    score_shape = (N_ROW, N_COL, depth, N_COL)
    scores = jax.random.randint(key_perm, score_shape, 0, 1 << 20, dtype=jnp.int32) * N_COL + lax.broadcasted_iota(jnp.int32, score_shape, 3)
    order = jnp.argsort(scores, axis=3).astype(jnp.int32).reshape(N_ROW, N_COL, depth * N_COL)[:, :, :KMAX]
    shape = (N_ROW, N_COL, KMAX)
    group_row = lax.broadcasted_iota(jnp.int32, shape, 0)
    group_col = lax.broadcasted_iota(jnp.int32, shape, 1)
    slot_index = lax.broadcasted_iota(jnp.int32, shape, 2)
    level = slot_index // N_COL
    rem_row = jax.random.randint(key_rem_row, shape, 0, BPD, dtype=jnp.int32)
    rem_col = jax.random.randint(key_rem_col, shape, 0, BPD, dtype=jnp.int32)
    marked = (group_col == 0) & (level == 0) & ((group_row == 0) | (group_row == N_ROW - 1))
    rem_row = jnp.where(marked, BPD - 1, rem_row)
    rem_col = jnp.where(marked, BPD - 1, rem_col)
    offset = jax.random.randint(key_offset, shape, 0, N_ROW, dtype=jnp.int32)
    offset = jnp.where(slot_index == 0, N_ROW // 2, offset)
    offset = jnp.where(slot_index == 1, N_ROW - 1, offset)
    offset = jnp.where(slot_index == 2, 1, offset)
    local_row = order * BPD + rem_row
    local_col = (group_row + offset) % N_ROW * BPD + rem_col
    live = (jax.random.randint(key_live, shape, 0, 4, dtype=jnp.int32) > 0) | (level == 0)
    live = live & jnp.logical_not((group_row == 0) & (group_col == 0) & (slot_index == KMAX - 1))
    empty = jnp.full(shape, -1, jnp.int32)
    return (jnp.where(live, local_row, empty).astype(jnp.int32), jnp.where(live, local_col, empty).astype(jnp.int32))


def draw_tile_row(key, part):
    rows, cols = shared_pattern(key)
    return rows


def draw_tile_col(key, part):
    rows, cols = shared_pattern(key)
    return cols


def steps_of(rng, shape, cuts, smallest, top_value):
    loudness = 1.0
    for dim, shards_of in cuts:
        draws = jax.random.uniform(jax.random.fold_in(jax.random.fold_in(rng, 6), dim), (shards_of,), jnp.float32, smallest / len(cuts), top_value / len(cuts))
        loudness = loudness * jnp.repeat(jnp.exp(draws), shape[dim] // shards_of).reshape((-1,) + (1,) * (len(shape) - 1 - dim))
    return loudness


def centred(key, shape, width, reach, pieces=(), kind=jnp.bfloat16):
    entries = width * jax.random.normal(key, shape, jnp.float32)
    if pieces:
        entries = entries * steps_of(key, shape, pieces, -0.22, 0.18)
    return jnp.clip(entries, -reach, reach).astype(kind)


def setup_inputs(seed: int = 0) -> dict:
    keys = jax.random.split(jax.random.key(seed), 5)
    vectors = centred(keys[0], (V, N), 1.0, 6.0, ((1, 512),))
    tiles = centred(keys[1], (N_ROW, N_COL, KMAX, B, B), (2 * TILES_ROW * B) ** -0.5, 0.078125, ((0, 32), (1, 16)))
    tile_row = draw_tile_row(jax.random.fold_in(keys[4], 71), 0)
    tile_col = draw_tile_col(jax.random.fold_in(keys[4], 71), 0)
    return {"vectors": vectors, "tiles": tiles, "tile_row": tile_row, "tile_col": tile_col}


CENTER = 0.5
HALF_WIDTH = 1.5


def block_indices(tile_row, tile_col):
    group_row = lax.broadcasted_iota(jnp.int32, tile_row.shape, 0)
    group_col = lax.broadcasted_iota(jnp.int32, tile_row.shape, 1)
    valid = tile_row >= 0
    local_row = jnp.maximum(tile_row, 0)
    local_col = jnp.maximum(tile_col, 0)
    global_row = group_row * (N_COL * BPD) + local_row
    global_col = ((local_col // BPD) * N_COL + group_col) * BPD + local_col % BPD
    return global_row.astype(jnp.int32), global_col.astype(jnp.int32), valid


def apply_hamiltonian(blocked, tiles, global_row, global_col, valid):
    count = N_COL * KMAX
    tile_sets = tiles.reshape(N_ROW, count, B, B)
    rows_all = global_row.reshape(N_ROW, count)
    cols_all = global_col.reshape(N_ROW, count)
    mask_all = valid.reshape(N_ROW, count)

    def one_group(total, parts):
        tile_set, rows, cols, okay = parts
        weight = okay.astype(jnp.float32)[None, :, None]
        left_rows = jnp.take(blocked, rows, axis=1).astype(jnp.float32)
        left_cols = jnp.take(blocked, cols, axis=1).astype(jnp.float32)
        tile_f = tile_set.astype(jnp.float32)
        to_cols = jnp.einsum("vka,kab->vkb", left_rows, tile_f, precision=lax.Precision.HIGHEST) * weight
        to_rows = jnp.einsum("vkb,kab->vka", left_cols, tile_f, precision=lax.Precision.HIGHEST) * weight
        total = total.at[:, cols].add(to_cols)
        total = total.at[:, rows].add(to_rows)
        return total, None

    start = jnp.zeros((V, NB, B), jnp.float32)
    total, unused = lax.scan(one_group, start, (tile_sets, rows_all, cols_all, mask_all))
    return total


def reference(vectors, tiles, tile_row, tile_col):
    global_row, global_col, valid = block_indices(tile_row, tile_col)
    blocked = vectors.reshape(V, NB, B)
    hx = apply_hamiltonian(blocked, tiles, global_row, global_col, valid)
    first = ((hx - CENTER * blocked.astype(jnp.float32)) / HALF_WIDTH).astype(jnp.bfloat16)
    hy = apply_hamiltonian(first, tiles, global_row, global_col, valid)
    second = 2.0 * (hy - CENTER * first.astype(jnp.float32)) / HALF_WIDTH - blocked.astype(jnp.float32)
    return first.reshape(V, N), second.reshape(V, N)
```

```python
import functools

import jax
import jax.numpy as jnp
from jax import lax
from jax.experimental import pallas as pl
from jax.experimental.pallas import tpu as pltpu
from jax.sharding import PartitionSpec as P

CENTER = 0.5
HALF_WIDTH = 1.5
MESH = pl.DeviceIdType.MESH


def filter_kernel(
    n_row,
    n_col,
    slots,
    trow,
    tcol,
    x_ref,
    tiles_hbm,
    first_ref,
    second_ref,
    tiles,
    y_ref,
    rowx0,
    rowx1,
    colx0,
    colx1,
    part_c,
    part_r,
    swap_out,
    swap_in,
    out_c,
    out_r,
    in_c,
    in_r,
    slot_of_row,
    extra_of_row,
    prev_slot,
    last_slot,
    tiles_sem,
    send_gr,
    recv_gr,
    send_gc,
    recv_gc,
    send_fw,
    recv_fw,
    send_sw,
    recv_sw,
    send_sc,
    recv_sc,
    send_sr,
    recv_sr,
):
    r = lax.axis_index("row")
    c = lax.axis_index("col")
    chips = n_row // 2
    m = r // 2
    core = r - 2 * m
    partner = r + 1 - 2 * core
    zero_slot = slots
    rowx = (rowx0, rowx1)
    colx = (colx0, colx1)

    def row_peer(k):
        return lax.rem(c + k, n_col)

    def row_source(k):
        return lax.rem(c + n_col - k, n_col)

    def col_peer(k):
        return 2 * lax.rem(m + k, chips) + core

    def col_source(k):
        return 2 * lax.rem(m + chips - k, chips) + core

    tiles_copy = pltpu.make_async_copy(tiles_hbm, tiles, tiles_sem)
    tiles_copy.start()

    barrier = pltpu.get_barrier_semaphore()

    def hello_row(k, _):
        pl.semaphore_signal(barrier, inc=1, device_id=(r, row_peer(k)), device_id_type=MESH)
        return 0

    def hello_col(k, _):
        pl.semaphore_signal(barrier, inc=1, device_id=(col_peer(k), c), device_id_type=MESH)
        return 0

    lax.fori_loop(1, n_col, hello_row, 0)
    lax.fori_loop(1, chips, hello_col, 0)
    pl.semaphore_signal(barrier, inc=1, device_id=(partner, c), device_id_type=MESH)
    pl.semaphore_wait(barrier, n_col - 1 + chips - 1 + 1)

    def remote(src, dst, send, recv, row, col):
        return pltpu.make_async_remote_copy(
            src_ref=src, dst_ref=dst, send_sem=send, recv_sem=recv, device_id=(row, col), device_id_type=MESH
        )

    def gather_row(a, src, k):
        return remote(src, rowx[a].at[c], send_gr.at[a, k], recv_gr.at[a, k], r, row_peer(k))

    def gather_col(a, src, k):
        return remote(src, colx[a].at[r], send_gc.at[a, k], recv_gc.at[a, k], col_peer(k), c)

    def forward(a, src, k):
        return remote(src, colx[a].at[col_source(k)], send_fw.at[a, k], recv_fw.at[a, k], partner, c)

    def swap(a):
        return remote(swap_out, swap_in.at[a], send_sw.at[a], recv_sw.at[a], partner, c)

    def scatter_col(a, k):
        return remote(
            out_c.at[lax.rem(m + k, chips)], in_c.at[a, k], send_sc.at[a, k], recv_sc.at[a, k], col_peer(k), c
        )

    def scatter_row(a, k):
        return remote(out_r.at[row_peer(k)], in_r.at[a, k], send_sr.at[a, k], recv_sr.at[a, k], r, row_peer(k))

    def tables():
        def rows(p, _):
            one = jnp.int32(0)
            for s in range(n_col):
                one = jnp.where(trow[s] == p, s, one)
            two = jnp.int32(zero_slot)
            for s in range(n_col, slots):
                two = jnp.where(trow[s] == p, s, two)
            slot_of_row[p] = one
            extra_of_row[p] = two
            return 0

        lax.fori_loop(0, n_col, rows, 0)
        for s in range(slots):
            here = jnp.int32(zero_slot)
            for t in range(s):
                here = jnp.where(tcol[t] == tcol[s], t, here)
            prev_slot[s] = here

        def cols(q, _):
            here = jnp.int32(zero_slot)
            for s in range(slots):
                here = jnp.where(tcol[s] == q, s, here)
            last_slot[q] = here
            return 0

        lax.fori_loop(0, n_row, cols, 0)

    def apply(a, src):
        def start_gather(k, _):
            gather_row(a, src, k).start()
            gather_col(a, src, k).start()
            return 0

        forward(a, src, 0).start()
        lax.fori_loop(1, n_col, start_gather, 0)
        rowx[a][c] = src[...]
        colx[a][r] = src[...]
        if a == 0:
            part_c[zero_slot] = jnp.zeros(part_c.shape[1:], part_c.dtype)
            part_r[zero_slot] = jnp.zeros(part_r.shape[1:], part_r.dtype)
            tables()
            tiles_copy.wait()

        def pass_on(k, _):
            gather_col(a, src, k).wait_recv()
            forward(a, colx[a].at[col_source(k)], k).start()
            return 0

        lax.fori_loop(1, chips, pass_on, 0)

        def wait_row(k, _):
            gather_row(a, src, k).wait_recv()
            return 0

        lax.fori_loop(1, n_col, wait_row, 0)

        for s in range(slots):
            left = rowx[a][jnp.maximum(trow[s], 0)]
            part_c[s] = jnp.dot(left, tiles[s], preferred_element_type=jnp.float32)
        for s in range(slots):
            part_c[s] = part_c[s] + part_c[prev_slot[s]]

        if a == 1:
            swap(0).wait_send()

        def fill_swap(k, _):
            swap_out[k] = part_c[last_slot[2 * k + 1 - core]]
            return 0

        lax.fori_loop(0, chips, fill_swap, 0)
        swap(a).start()

        def wait_forward(k, _):
            forward(a, src, k).wait_recv()
            return 0

        lax.fori_loop(0, chips, wait_forward, 0)

        for s in range(slots):
            left = colx[a][jnp.maximum(tcol[s], 0)]
            part_r[s] = lax.dot_general(
                left, tiles[s], (((1,), (1,)), ((), ())), preferred_element_type=jnp.float32
            )

        if a == 1:

            def sent(k, _):
                scatter_row(0, k).wait_send()
                scatter_col(0, k).wait_send()
                return 0

            lax.fori_loop(1, n_col, sent, 0)

        def fill_row(k, _):
            p = row_peer(k)
            out_r[p] = part_r[slot_of_row[p]] + part_r[extra_of_row[p]]

            @pl.when(k < n_col)
            def _():
                scatter_row(a, k).start()

            return 0

        lax.fori_loop(1, n_col + 1, fill_row, 0)
        swap(a).wait_recv()

        def fill_col(k, _):
            q = lax.rem(m + k, chips)
            out_c[q] = part_c[last_slot[2 * q + core]] + swap_in[a, q]

            @pl.when(k < chips)
            def _():
                scatter_col(a, k).start()

            return 0

        lax.fori_loop(1, chips + 1, fill_col, 0)

        def add(k, total):
            scatter_row(a, k).wait_recv()
            scatter_col(a, k).wait_recv()
            return total + (in_r[a, k] + in_c[a, k])

        return lax.fori_loop(1, n_col, add, out_r[c] + out_c[m])

    x = x_ref[...].astype(jnp.float32)
    hx = apply(0, x_ref)
    y_ref[...] = ((hx - CENTER * x) / HALF_WIDTH).astype(jnp.bfloat16)
    hy = apply(1, y_ref)
    y = y_ref[...]
    first_ref[...] = y
    second_ref[...] = 2.0 * (hy - CENTER * y.astype(jnp.float32)) / HALF_WIDTH - x

    swap(1).wait_send()

    def drain(k, _):
        gather_row(0, x_ref, k).wait_send()
        gather_col(0, x_ref, k).wait_send()
        gather_row(1, y_ref, k).wait_send()
        gather_col(1, y_ref, k).wait_send()
        scatter_row(1, k).wait_send()
        scatter_col(1, k).wait_send()
        return 0

    lax.fori_loop(1, n_col, drain, 0)

    def drain_forward(k, _):
        forward(0, x_ref, k).wait_send()
        forward(1, y_ref, k).wait_send()
        return 0

    lax.fori_loop(0, chips, drain_forward, 0)


def shards(vectors, tiles, tile_row, tile_col):
    n_row = lax.axis_size("row")
    n_col = lax.axis_size("col")
    slots = tiles.shape[2]
    block = tiles.shape[-1]
    count = vectors.shape[0]
    chips = n_row // 2
    f32, bf16 = jnp.float32, jnp.bfloat16
    dma = pltpu.SemaphoreType.DMA
    vmem = pl.BlockSpec(memory_space=pltpu.VMEM)
    smem = pl.BlockSpec(memory_space=pltpu.SMEM)
    return pl.pallas_call(
        functools.partial(filter_kernel, n_row, n_col, slots),
        out_shape=(
            jax.ShapeDtypeStruct((count, block), bf16),
            jax.ShapeDtypeStruct((count, block), f32),
        ),
        in_specs=[smem, smem, vmem, pl.BlockSpec(memory_space=pl.ANY)],
        out_specs=(vmem, vmem),
        scratch_shapes=[
            pltpu.VMEM((slots, block, block), bf16),
            pltpu.VMEM((count, block), bf16),
            pltpu.VMEM((n_col, count, block), bf16),
            pltpu.VMEM((n_col, count, block), bf16),
            pltpu.VMEM((n_row, count, block), bf16),
            pltpu.VMEM((n_row, count, block), bf16),
            pltpu.VMEM((slots + 1, count, block), f32),
            pltpu.VMEM((slots + 1, count, block), f32),
            pltpu.VMEM((chips, count, block), f32),
            pltpu.VMEM((2, chips, count, block), f32),
            pltpu.VMEM((chips, count, block), f32),
            pltpu.VMEM((n_col, count, block), f32),
            pltpu.VMEM((2, chips, count, block), f32),
            pltpu.VMEM((2, n_col, count, block), f32),
            pltpu.SMEM((n_col,), jnp.int32),
            pltpu.SMEM((n_col,), jnp.int32),
            pltpu.SMEM((slots,), jnp.int32),
            pltpu.SMEM((n_row,), jnp.int32),
            dma(()),
            dma((2, n_col)),
            dma((2, n_col)),
            dma((2, chips)),
            dma((2, chips)),
            dma((2, chips)),
            dma((2, chips)),
            dma((2,)),
            dma((2,)),
            dma((2, chips)),
            dma((2, chips)),
            dma((2, n_col)),
            dma((2, n_col)),
        ],
        compiler_params=pltpu.CompilerParams(
            collective_id=0, has_side_effects=True, vmem_limit_bytes=32 * 1024 * 1024
        ),
        cost_estimate=pl.CostEstimate(
            flops=8 * slots * count * block * block, bytes_accessed=2 * slots * block * block, transcendentals=0
        ),
    )(tile_row[0, 0], tile_col[0, 0], vectors, tiles[0, 0])


def solution(mesh):
    placed = (
        P(None, ("row", "col")),
        P("row", "col", None, None, None),
        P("row", "col", None),
        P("row", "col", None),
    )
    return jax.shard_map(
        shards,
        mesh=mesh,
        in_specs=placed,
        out_specs=(P(None, ("row", "col")), P(None, ("row", "col"))),
        check_vma=False,
    )
```

```python
import functools

import jax
import jax.numpy as jnp
from jax import lax
from jax.experimental import pallas as pl
from jax.experimental.pallas import tpu as pltpu
from jax.sharding import PartitionSpec as P

CENTER = 0.5
HALF_WIDTH = 1.5
MESH = pl.DeviceIdType.MESH
PARTS = 2

LIMITS = (2.0**12, 2.0**24)
TINY = 1e-30


def encode(v, limit):
    root = lax.rsqrt(lax.rsqrt(lax.rsqrt(lax.rsqrt(jnp.maximum(jnp.abs(v), TINY)))))
    code = root * (32767.0 / limit ** (1 / 16)) + 0.5
    code = jnp.where(jnp.abs(v) <= TINY, 0.0, code)
    return jnp.where(v < 0, -code, code).astype(jnp.int32).astype(jnp.int16)


def decode(code, limit):
    code = code.astype(jnp.int32).astype(jnp.float32)
    root = code * (limit ** (1 / 16) / 32767.0)
    power = root * root
    power = power * power
    power = power * power
    power = power * power
    return jnp.where(code < 0, -power, power)


def filter_kernel(n_row, n_col, slots, trow_hbm, tcol_hbm, x_hbm, tiles_hbm, first_ref, second_ref, *scratch):
    (
        trow_ref, tcol_ref, x_ref, tiles, y_ref, part_c, part_r, swap_out, swap_in, out_c, out_r, in_c, in_r,
        slot_of_row, extra_of_row, prev_slot, last_slot, fetch_sem,
        send_gr, recv_gr, send_gc, recv_gc, send_fw, recv_fw, send_sw, recv_sw, send_sc, recv_sc, send_sr, recv_sr,
    ) = scratch[:30]
    rowx = (scratch[30 : 30 + PARTS], scratch[30 + PARTS : 30 + 2 * PARTS])
    colx = (scratch[30 + 2 * PARTS : 30 + 3 * PARTS], scratch[30 + 3 * PARTS :])
    r = lax.axis_index("row")
    c = lax.axis_index("col")
    chips = n_row // 2
    assert chips == n_col
    ring = n_col // 2
    m = r // 2
    core = r - 2 * m
    partner = r + 1 - 2 * core
    zero_slot = slots
    height = x_ref.shape[0] // PARTS

    def offset(k):
        i = k // 2
        j = (i + 1) // 2
        return ring // 2 + j * (1 - 2 * (i % 2)), 1 - k % 2

    def peer(index, k):
        d, x = offset(k)
        return 2 * lax.rem(index // 2 + d, ring) + lax.rem(index % 2 + x, 2)

    def source(index, k):
        d, x = offset(k)
        return 2 * lax.rem(index // 2 + ring - d, ring) + lax.rem(index % 2 + x, 2)

    def row_peer(k):
        return peer(c, k)

    def col_peer(k):
        return 2 * peer(m, k) + core

    def col_source(k):
        return 2 * source(m, k) + core

    def fetch(i, src, dst):
        return pltpu.make_async_copy(src, dst, fetch_sem.at[i])

    fetch_x = fetch(0, x_hbm, x_ref)
    fetch_row = fetch(1, trow_hbm, trow_ref)
    fetch_col = fetch(2, tcol_hbm, tcol_ref)
    fetch_tiles = fetch(3, tiles_hbm, tiles)
    fetch_x.start()

    barrier = pltpu.get_barrier_semaphore()

    def hello(k, _):
        pl.semaphore_signal(barrier, inc=1, device_id=(r, row_peer(k)), device_id_type=MESH)
        pl.semaphore_signal(barrier, inc=1, device_id=(col_peer(k), c), device_id_type=MESH)
        return 0

    lax.fori_loop(0, n_col - 1, hello, 0)
    pl.semaphore_signal(barrier, inc=1, device_id=(partner, c), device_id_type=MESH)
    fetch_row.start()
    fetch_col.start()
    fetch_tiles.start()
    fetch_x.wait()
    pl.semaphore_wait(barrier, 2 * (n_col - 1) + 1)

    def remote(src, dst, send, recv, row, col):
        return pltpu.make_async_remote_copy(
            src_ref=src, dst_ref=dst, send_sem=send, recv_sem=recv, device_id=(row, col), device_id_type=MESH
        )

    def rows_of(h):
        return pl.ds(h * height, height)

    current = (x_ref, y_ref)

    def gather_row(a, h, k):
        src = current[a].at[rows_of(h)]
        return remote(src, rowx[a][h].at[c], send_gr.at[a, h, k], recv_gr.at[a, h, k], r, row_peer(k))

    def gather_col(a, h, k):
        src = current[a].at[rows_of(h)]
        return remote(src, colx[a][h].at[r], send_gc.at[a, h, k], recv_gc.at[a, h, k], col_peer(k), c)

    def forward(a, h, k):
        block = colx[a][h].at[col_source(k)]
        return remote(block, block, send_fw.at[a, h, k], recv_fw.at[a, h, k], partner, c)

    def swap(a, h):
        return remote(swap_out.at[a, h], swap_in.at[a, h], send_sw.at[a, h], recv_sw.at[a, h], partner, c)

    def scatter_col(a, h, k):
        return remote(
            out_c.at[a, h, k], in_c.at[a, h, k], send_sc.at[a, h, k], recv_sc.at[a, h, k], col_peer(k), c
        )

    def scatter_row(a, h, k):
        return remote(
            out_r.at[a, h, k], in_r.at[a, h, k], send_sr.at[a, h, k], recv_sr.at[a, h, k], r, row_peer(k)
        )

    def trow(s):
        return trow_ref[0, s]

    def tcol(s):
        return tcol_ref[0, s]

    def tables():
        part_c[zero_slot] = jnp.zeros(part_c.shape[1:], part_c.dtype)
        part_r[zero_slot] = jnp.zeros(part_r.shape[1:], part_r.dtype)

        def rows(p, _):
            one = jnp.int32(0)
            for s in range(n_col):
                one = jnp.where(trow(s) == p, s, one)
            two = jnp.int32(zero_slot)
            for s in range(n_col, slots):
                two = jnp.where(trow(s) == p, s, two)
            slot_of_row[p] = one
            extra_of_row[p] = two
            return 0

        lax.fori_loop(0, n_col, rows, 0)
        for s in range(slots):
            here = jnp.int32(zero_slot)
            for t in range(s):
                here = jnp.where(tcol(t) == tcol(s), t, here)
            prev_slot[s] = here

        def cols(q, _):
            here = jnp.int32(zero_slot)
            for s in range(slots):
                here = jnp.where(tcol(s) == q, s, here)
            last_slot[q] = here
            return 0

        lax.fori_loop(0, n_row, cols, 0)

    def start_gather(a, h):
        def start(k, _):
            gather_row(a, h, k).start()
            gather_col(a, h, k).start()
            return 0

        lax.fori_loop(0, n_col - 1, start, 0)
        block = current[a][rows_of(h)]
        rowx[a][h][c] = block
        colx[a][h][r] = block
        forward(a, h, n_col - 1).start()

    def products(a, h):
        def pass_on(k, _):
            gather_col(a, h, k).wait_recv()
            forward(a, h, k).start()
            return 0

        lax.fori_loop(0, chips - 1, pass_on, 0)

        def wait_row(k, _):
            gather_row(a, h, k).wait_recv()
            return 0

        lax.fori_loop(0, n_col - 1, wait_row, 0)
        for s in range(slots):
            left = rowx[a][h][jnp.maximum(trow(s), 0)]
            part_c[s] = jnp.dot(left, tiles[s], preferred_element_type=jnp.float32)
        for s in range(slots):
            part_c[s] = part_c[s] + part_c[prev_slot[s]]

        def fill_swap(k, _):
            swap_out[a, h, k] = part_c[last_slot[2 * k + 1 - core]]
            return 0

        lax.fori_loop(0, chips, fill_swap, 0)
        swap(a, h).start()

        def wait_forward(k, _):
            forward(a, h, k).wait_recv()
            return 0

        lax.fori_loop(0, chips, wait_forward, 0)
        for s in range(slots):
            left = colx[a][h][jnp.maximum(tcol(s), 0)]
            part_r[s] = lax.dot_general(
                left, tiles[s], (((1,), (1,)), ((), ())), preferred_element_type=jnp.float32
            )

        def row_sum(p):
            return part_r[slot_of_row[p]] + part_r[extra_of_row[p]]

        def col_sum(q):
            return part_c[last_slot[2 * q + core]] + swap_in[a, h, q]

        def send_row(k, _):
            out_r[a, h, k] = encode(row_sum(row_peer(k)), LIMITS[a])
            scatter_row(a, h, k).start()
            return 0

        lax.fori_loop(0, n_col - 1, send_row, 0)
        swap(a, h).wait_recv()

        def send_col(k, _):
            out_c[a, h, k] = encode(col_sum(peer(m, k)), LIMITS[a])
            scatter_col(a, h, k).start()
            return 0

        lax.fori_loop(0, chips - 1, send_col, 0)
        return row_sum(c) + col_sum(m)

    def collect(a, h, total):
        def add(k, total):
            scatter_row(a, h, k).wait_recv()
            scatter_col(a, h, k).wait_recv()
            return total + (decode(in_r[a, h, k], LIMITS[a]) + decode(in_c[a, h, k], LIMITS[a]))

        return lax.fori_loop(0, n_col - 1, add, total)

    parts = range(PARTS)
    for h in parts:
        start_gather(0, h)
    fetch_row.wait()
    fetch_col.wait()
    tables()
    fetch_tiles.wait()
    own = [products(0, h) for h in parts]
    for h in parts:
        hx = collect(0, h, own[h])
        x = x_ref[rows_of(h)].astype(jnp.float32)
        y_ref[rows_of(h)] = ((hx - CENTER * x) / HALF_WIDTH).astype(jnp.bfloat16)
        start_gather(1, h)
    own = [products(1, h) for h in parts]
    for h in parts:
        hy = collect(1, h, own[h])
        x = x_ref[rows_of(h)].astype(jnp.float32)
        y = y_ref[rows_of(h)]
        first_ref[rows_of(h)] = y
        second_ref[rows_of(h)] = 2.0 * (hy - CENTER * y.astype(jnp.float32)) / HALF_WIDTH - x

    for a in range(2):
        for h in parts:
            swap(a, h).wait_send()
            forward(a, h, n_col - 1).wait_send()

            def drain(k, _):
                gather_row(a, h, k).wait_send()
                gather_col(a, h, k).wait_send()
                forward(a, h, k).wait_send()
                scatter_row(a, h, k).wait_send()
                scatter_col(a, h, k).wait_send()
                return 0

            lax.fori_loop(0, n_col - 1, drain, 0)


def shards(vectors, tiles, tile_row, tile_col):
    n_row = lax.axis_size("row")
    n_col = lax.axis_size("col")
    slots = tiles.shape[2]
    block = tiles.shape[-1]
    count = vectors.shape[0]
    chips = n_row // 2
    height = count // PARTS
    f32, bf16, i16 = jnp.float32, jnp.bfloat16, jnp.int16
    dma = pltpu.SemaphoreType.DMA
    vmem = pl.BlockSpec(memory_space=pltpu.VMEM)
    hbm = pl.BlockSpec(memory_space=pltpu.HBM)
    return pl.pallas_call(
        functools.partial(filter_kernel, n_row, n_col, slots),
        out_shape=(
            jax.ShapeDtypeStruct((count, block), bf16),
            jax.ShapeDtypeStruct((count, block), f32),
        ),
        in_specs=[hbm] * 4,
        out_specs=(vmem, vmem),
        scratch_shapes=[
            pltpu.SMEM((1, slots), jnp.int32),
            pltpu.SMEM((1, slots), jnp.int32),
            pltpu.VMEM((count, block), bf16),
            pltpu.VMEM((slots, block, block), bf16),
            pltpu.VMEM((count, block), bf16),
            pltpu.VMEM((slots + 1, height, block), f32),
            pltpu.VMEM((slots + 1, height, block), f32),
            pltpu.VMEM((2, PARTS, chips, height, block), f32),
            pltpu.VMEM((2, PARTS, chips, height, block), f32),
            pltpu.VMEM((2, PARTS, chips, height, block), i16),
            pltpu.VMEM((2, PARTS, n_col, height, block), i16),
            pltpu.VMEM((2, PARTS, chips, height, block), i16),
            pltpu.VMEM((2, PARTS, n_col, height, block), i16),
            pltpu.SMEM((n_col,), jnp.int32),
            pltpu.SMEM((n_col,), jnp.int32),
            pltpu.SMEM((slots,), jnp.int32),
            pltpu.SMEM((n_row,), jnp.int32),
            dma((4,)),
        ]
        + [dma((2, PARTS, n_col))] * 6
        + [dma((2, PARTS))] * 2
        + [dma((2, PARTS, n_col))] * 4
        + [pltpu.VMEM((n_col, height, block), bf16)] * (2 * PARTS)
        + [pltpu.VMEM((n_row, height, block), bf16)] * (2 * PARTS),
        compiler_params=pltpu.CompilerParams(
            collective_id=0, has_side_effects=True, vmem_limit_bytes=48 * 1024 * 1024
        ),
        cost_estimate=pl.CostEstimate(
            flops=8 * slots * count * block * block, bytes_accessed=2 * slots * block * block, transcendentals=0
        ),
    )(tile_row[0], tile_col[0], vectors, tiles[0, 0])


def solution(mesh):
    placed = (
        P(None, ("row", "col")),
        P("row", "col", None, None, None),
        P("row", "col", None),
        P("row", "col", None),
    )
    return jax.shard_map(
        shards,
        mesh=mesh,
        in_specs=placed,
        out_specs=(P(None, ("row", "col")), P(None, ("row", "col"))),
        check_vma=False,
    )
```

```python
import functools

import jax
import jax.numpy as jnp
from jax import lax
from jax.experimental import pallas as pl
from jax.experimental.pallas import tpu as pltpu
from jax.sharding import PartitionSpec as P

CENTER = 0.5
HALF_WIDTH = 1.5
MESH = pl.DeviceIdType.MESH
BATCH = 4
PARTS = 2

LIMITS = (2.0**12, 2.0**24)
SCALES = tuple(32767.0 / limit ** (1 / 16) for limit in LIMITS)
TINY = 1e-30
GROUP = 5


def encode(v, scale):
    root = lax.rsqrt(lax.rsqrt(lax.rsqrt(lax.rsqrt(jnp.maximum(jnp.abs(v), TINY)))))
    code = jnp.where(jnp.abs(v) <= TINY, 0.0, root * scale + 0.5)
    return jnp.where(v < 0, -code, code).astype(jnp.int32).astype(jnp.int16)


def decode(code, scale):
    code = code.astype(jnp.int32).astype(jnp.float32)
    power = code * scale
    power = power * power
    power = power * power
    power = power * power
    power = power * power
    return jnp.where(code < 0, -power, power)


def filter_kernel(n_row, n_col, slots, trow_hbm, tcol_hbm, x_hbm, tiles_hbm, first_ref, second_ref, *scratch):
    (
        trow_ref, tcol_ref, tiles, current, own, row_now, col_now, rowx, colx, part_c, part_r, swap_out, swap_in,
        out_c, out_r, in_c, in_r, slot_of_row, extra_of_row, prev_slot, last_slot, place_of_chip, row_place, col_place,
        fetch_sem, send_gr, recv_gr, send_gc, recv_gc, send_sc, recv_sc, send_sr, recv_sr,
        send_fw, recv_fw, send_sw, recv_sw,
    ) = scratch
    r = lax.axis_index("row")
    c = lax.axis_index("col")
    chips = n_row // 2
    assert chips == n_col
    ring = n_col // 2
    m = r // 2
    core = r - 2 * m
    partner = r + 1 - 2 * core
    zero_slot = slots
    height = current.shape[1] // PARTS
    peers = n_col - 1

    def loop(count, body, unroll=1):
        def step(k, _):
            body(k)
            return 0

        lax.fori_loop(0, count, step, 0, unroll=unroll)

    def offset(k):
        i = k // 2
        j = (i + 1) // 2
        return ring // 2 + j * (1 - 2 * (i % 2)), 1 - k % 2

    def peer(index, k):
        d, x = offset(k)
        return 2 * lax.rem(index // 2 + d, ring) + lax.rem(index % 2 + x, 2)

    def source(index, k):
        d, x = offset(k)
        return 2 * lax.rem(index // 2 + ring - d, ring) + lax.rem(index % 2 + x, 2)

    def row_peer(k):
        return peer(c, k)

    def col_peer(k):
        return 2 * peer(m, k) + core

    def fetch(i, src, dst):
        return pltpu.make_async_copy(src, dst, fetch_sem.at[i])

    fetch_x = fetch(0, x_hbm, current.at[0])
    fetch_row = fetch(1, trow_hbm, trow_ref)
    fetch_col = fetch(2, tcol_hbm, tcol_ref)
    fetch_tiles = fetch(3, tiles_hbm, tiles)
    fetch_x.start()

    barrier = pltpu.get_barrier_semaphore()

    @functools.partial(loop, peers)
    def _(k):
        pl.semaphore_signal(barrier, inc=1, device_id=(r, row_peer(k)), device_id_type=MESH)
        pl.semaphore_signal(barrier, inc=1, device_id=(col_peer(k), c), device_id_type=MESH)

    pl.semaphore_signal(barrier, inc=1, device_id=(partner, c), device_id_type=MESH)
    fetch_row.start()
    fetch_col.start()
    fetch_tiles.start()
    fetch_x.wait()
    pl.semaphore_wait(barrier, 2 * peers + 1)

    def remote(src, dst, send, recv, row, col):
        return pltpu.make_async_remote_copy(
            src_ref=src, dst_ref=dst, send_sem=send, recv_sem=recv, device_id=(row, col), device_id_type=MESH
        )

    def rows_of(h):
        return pl.ds(pl.multiple_of(h * height, height), height)

    def gather_row(a, h, k):
        src = current.at[a, rows_of(h)]
        return remote(src, rowx.at[a, h, k], send_gr.at[a, h, k], recv_gr.at[a, h, k], r, row_peer(k))

    def gather_col(a, h, k):
        src = current.at[a, rows_of(h)]
        dst = colx.at[a, h, core * chips + k]
        return remote(src, dst, send_gc.at[a, h, k], recv_gc.at[a, h, k], col_peer(k), c)

    def forward(a, h, j):
        blocks = colx.at[a, h, pl.ds(core * chips + j * BATCH, BATCH)]
        return remote(blocks, blocks, send_fw.at[a, h, j], recv_fw.at[a, h, j], partner, c)

    def swap(a, h, j):
        half = pl.ds(j * (chips // 2), chips // 2)
        return remote(
            swap_out.at[a, h, half], swap_in.at[a, h, half], send_sw.at[a, h, j], recv_sw.at[a, h, j], partner, c
        )

    def scatter_col(a, h, k):
        return remote(
            out_c.at[a, h, k], in_c.at[a, h, k], send_sc.at[a, h, k], recv_sc.at[a, h, k], col_peer(k), c
        )

    def scatter_row(a, h, k):
        return remote(
            out_r.at[a, h, k], in_r.at[a, h, k], send_sr.at[a, h, k], recv_sr.at[a, h, k], r, row_peer(k)
        )

    def trow(s):
        return trow_ref[0, s]

    def tcol(s):
        return tcol_ref[0, s]

    def tables():
        part_c[zero_slot] = jnp.zeros(part_c.shape[1:], part_c.dtype)
        part_r[zero_slot] = jnp.zeros(part_r.shape[1:], part_r.dtype)

        @functools.partial(loop, n_col)
        def _(p):
            one = jnp.int32(0)
            for s in range(n_col):
                one = jnp.where(trow(s) == p, s, one)
            two = jnp.int32(zero_slot)
            for s in range(n_col, slots):
                two = jnp.where(trow(s) == p, s, two)
            slot_of_row[p] = one
            extra_of_row[p] = two

        @functools.partial(loop, n_row)
        def _(q):
            here = jnp.int32(zero_slot)
            for s in range(slots):
                here = jnp.where(tcol(s) == q, s, here)
            last_slot[q] = here

        @functools.partial(loop, chips)
        def _(k):
            place_of_chip[source(m, k)] = k
            row_place[source(c, k)] = k

        @functools.partial(loop, slots)
        def _(s):
            here = jnp.int32(zero_slot)
            for t in range(slots):
                here = jnp.where((tcol(t) == tcol(s)) & (t < s), t, here)
            prev_slot[s] = here
            q = jnp.maximum(tcol(s), 0)
            col_place[s] = lax.rem(q, 2) * chips + place_of_chip[lax.div(q, 2)]

    def start_gather(a, h):
        @functools.partial(loop, peers)
        def _(k):
            gather_row(a, h, k).start()
            gather_col(a, h, k).start()

        block = current[a, rows_of(h)]
        rowx[a, h, n_col - 1] = block
        colx[a, h, core * chips + chips - 1] = block

    def products(a, h):
        scale = jnp.where(a == 0, SCALES[0], SCALES[1])

        @functools.partial(loop, chips // BATCH)
        def _(j):
            @functools.partial(loop, BATCH, unroll=True)
            def _(i):
                @pl.when(j * BATCH + i < peers)
                def _():
                    gather_col(a, h, j * BATCH + i).wait_recv()

            forward(a, h, j).start()

        @functools.partial(loop, peers, unroll=True)
        def _(k):
            gather_row(a, h, k).wait_recv()

        for k in range(n_col):
            row_now[k] = rowx[a, h, k]
        for s in range(slots):
            left = row_now[row_place[jnp.maximum(trow(s), 0)]]
            part_c[s] = jnp.dot(left, tiles[s], preferred_element_type=jnp.float32)
        for s in range(slots):
            part_c[s] = part_c[s] + part_c[prev_slot[s]]

        @functools.partial(loop, 2)
        def _(j):
            for i in range(chips // 2):
                k = j * (chips // 2) + i
                swap_out[a, h, k] = part_c[last_slot[2 * peer(m, k) + 1 - core]]

            swap(a, h, j).start()

        @functools.partial(loop, chips // BATCH)
        def _(j):
            forward(a, h, j).wait_recv()

        for k in range(n_row):
            col_now[k] = colx[a, h, k]
        for s in range(slots):
            part_r[s] = lax.dot_general(
                col_now[col_place[s]], tiles[s], (((1,), (1,)), ((), ())), preferred_element_type=jnp.float32
            )

        def row_sum(k):
            p = peer(c, k)
            return part_r[slot_of_row[p]] + part_r[extra_of_row[p]]

        def col_sum(k):
            return part_c[last_slot[2 * peer(m, k) + core]] + swap_in[a, h, k]

        def send(sums, out, copy):
            @functools.partial(loop, peers // GROUP)
            def _(g):
                for i in range(GROUP):
                    out[a, h, g * GROUP + i] = encode(sums(g * GROUP + i), scale)
                for i in range(GROUP):
                    copy(a, h, g * GROUP + i).start()

        send(row_sum, out_r, scatter_row)
        swap(a, h, 0).wait_recv()
        swap(a, h, 1).wait_recv()
        send(col_sum, out_c, scatter_col)
        own[h] = row_sum(n_col - 1) + col_sum(chips - 1)

    def collect(a, h):
        scale = jnp.where(a == 0, 1.0 / SCALES[0], 1.0 / SCALES[1])

        def add(g, total):
            for i in range(GROUP):
                scatter_row(a, h, g * GROUP + i).wait_recv()
                scatter_col(a, h, g * GROUP + i).wait_recv()
            for i in range(GROUP):
                k = g * GROUP + i
                total = total + (decode(in_r[a, h, k], scale) + decode(in_c[a, h, k], scale))
            return total

        return lax.fori_loop(0, peers // GROUP, add, own[h])

    @functools.partial(loop, 3)
    def _(a):
        @functools.partial(loop, PARTS)
        def _(h):
            @pl.when(a > 0)
            def _():
                total = collect(a - 1, h)
                before = current[a - 1, rows_of(h)].astype(jnp.float32)

                @pl.when(a == 1)
                def _():
                    first = ((total - CENTER * before) / HALF_WIDTH).astype(jnp.bfloat16)
                    current[1, rows_of(h)] = first
                    first_ref[rows_of(h)] = first

                @pl.when(a == 2)
                def _():
                    x = current[0, rows_of(h)].astype(jnp.float32)
                    second_ref[rows_of(h)] = 2.0 * (total - CENTER * before) / HALF_WIDTH - x

            @pl.when(a < 2)
            def _():
                start_gather(a, h)

        @pl.when(a == 0)
        def _():
            fetch_row.wait()
            fetch_col.wait()
            tables()
            fetch_tiles.wait()

        @pl.when(a < 2)
        def _():
            @functools.partial(loop, PARTS)
            def _(h):
                products(a, h)

    @functools.partial(loop, 2)
    def _(a):
        @functools.partial(loop, PARTS)
        def _(h):
            @functools.partial(loop, 2)
            def _(j):
                swap(a, h, j).wait_send()

            @functools.partial(loop, chips // BATCH)
            def _(j):
                forward(a, h, j).wait_send()

            @functools.partial(loop, peers)
            def _(k):
                gather_row(a, h, k).wait_send()
                gather_col(a, h, k).wait_send()
                scatter_row(a, h, k).wait_send()
                scatter_col(a, h, k).wait_send()


def shards(vectors, tiles, tile_row, tile_col):
    n_row = lax.axis_size("row")
    n_col = lax.axis_size("col")
    slots = tiles.shape[2]
    block = tiles.shape[-1]
    count = vectors.shape[0]
    chips = n_row // 2
    height = count // PARTS
    f32, bf16, i16 = jnp.float32, jnp.bfloat16, jnp.int16
    dma = pltpu.SemaphoreType.DMA
    vmem = pl.BlockSpec(memory_space=pltpu.VMEM)
    hbm = pl.BlockSpec(memory_space=pltpu.HBM)
    return pl.pallas_call(
        functools.partial(filter_kernel, n_row, n_col, slots),
        out_shape=(
            jax.ShapeDtypeStruct((count, block), bf16),
            jax.ShapeDtypeStruct((count, block), f32),
        ),
        in_specs=[hbm] * 4,
        out_specs=(vmem, vmem),
        scratch_shapes=[
            pltpu.SMEM((1, slots), jnp.int32),
            pltpu.SMEM((1, slots), jnp.int32),
            pltpu.VMEM((slots, block, block), bf16),
            pltpu.VMEM((2, count, block), bf16),
            pltpu.VMEM((PARTS, height, block), f32),
            pltpu.VMEM((n_col, height, block), bf16),
            pltpu.VMEM((n_row, height, block), bf16),
            pltpu.VMEM((2, PARTS, n_col, height, block), bf16),
            pltpu.VMEM((2, PARTS, n_row, height, block), bf16),
            pltpu.VMEM((slots + 1, height, block), f32),
            pltpu.VMEM((slots + 1, height, block), f32),
            pltpu.VMEM((2, PARTS, chips, height, block), f32),
            pltpu.VMEM((2, PARTS, chips, height, block), f32),
        ]
        + [pltpu.VMEM((2, PARTS, chips, height, block), i16)] * 4
        + [
            pltpu.SMEM((n_col,), jnp.int32),
            pltpu.SMEM((n_col,), jnp.int32),
            pltpu.SMEM((slots,), jnp.int32),
            pltpu.SMEM((n_row,), jnp.int32),
            pltpu.SMEM((chips,), jnp.int32),
            pltpu.SMEM((n_col,), jnp.int32),
            pltpu.SMEM((slots,), jnp.int32),
            dma((4,)),
        ]
        + [dma((2, PARTS, n_col))] * 8
        + [dma((2, PARTS, chips // BATCH))] * 2
        + [dma((2, PARTS, 2))] * 2,
        compiler_params=pltpu.CompilerParams(
            collective_id=0, has_side_effects=True, vmem_limit_bytes=64 * 1024 * 1024 - 4096
        ),
        cost_estimate=pl.CostEstimate(
            flops=8 * slots * count * block * block, bytes_accessed=2 * slots * block * block, transcendentals=0
        ),
    )(tile_row[0], tile_col[0], vectors, tiles[0, 0])


def solution(mesh):
    placed = (
        P(None, ("row", "col")),
        P("row", "col", None, None, None),
        P("row", "col", None),
        P("row", "col", None),
    )
    return jax.shard_map(
        shards,
        mesh=mesh,
        in_specs=placed,
        out_specs=(P(None, ("row", "col")), P(None, ("row", "col"))),
        check_vma=False,
    )
```

```python
import functools

import jax
import jax.numpy as jnp
from jax import lax
from jax.experimental import pallas as pl
from jax.experimental.pallas import tpu as pltpu
from jax.sharding import PartitionSpec as P

CENTER = 0.5
HALF_WIDTH = 1.5
MESH = pl.DeviceIdType.MESH
BATCH = 4
PARTS = 2

LIMITS = (2.0**12, 2.0**24)
SCALES = tuple(32767.0 / limit ** (1 / 16) for limit in LIMITS)
TINY = 1e-30
GROUP = 3


def encode(v, scale):
    root = lax.rsqrt(lax.rsqrt(lax.rsqrt(lax.rsqrt(jnp.maximum(jnp.abs(v), TINY)))))
    code = jnp.where(jnp.abs(v) <= TINY, 0.0, root * scale + 0.5)
    return jnp.where(v < 0, -code, code).astype(jnp.int32).astype(jnp.int16)


def decode(code, scale):
    code = code.astype(jnp.int32).astype(jnp.float32)
    power = code * scale
    power = power * power
    power = power * power
    power = power * power
    power = power * power
    return jnp.where(code < 0, -power, power)


def filter_kernel(n_row, n_col, slots, trow_hbm, tcol_hbm, x_hbm, tiles_hbm, first_ref, second_ref, *scratch):
    (
        trow_ref, tcol_ref, tiles, current, own, row_now, col_now, rowx, colx, part_c, part_r, swap_out, swap_in,
        out_c, out_r, in_c, in_r, row_slot, row_extra, prev_slot, own_last, other_last, place_of_chip, row_place,
        left_row, col_place,
        fetch_sem, send_gr, recv_gr, send_gc, recv_gc, send_sc, recv_sc, send_sr, recv_sr,
        send_fw, recv_fw, send_sw, recv_sw,
    ) = scratch
    r = lax.axis_index("row")
    c = lax.axis_index("col")
    chips = n_row // 2
    assert chips == n_col
    ring = n_col // 2
    m = r // 2
    core = r - 2 * m
    partner = r + 1 - 2 * core
    zero_slot = slots
    height = current.shape[1] // PARTS
    peers = n_col - 1

    def loop(count, body, unroll=1):
        def step(k, _):
            body(k)
            return 0

        lax.fori_loop(0, count, step, 0, unroll=unroll)

    def offset(k):
        i = k // 2
        j = (i + 1) // 2
        return ring // 2 + j * (1 - 2 * (i % 2)), 1 - k % 2

    def peer(index, k):
        d, x = offset(k)
        return 2 * lax.rem(index // 2 + d, ring) + lax.rem(index % 2 + x, 2)

    def source(index, k):
        d, x = offset(k)
        return 2 * lax.rem(index // 2 + ring - d, ring) + lax.rem(index % 2 + x, 2)

    def row_peer(k):
        return peer(c, k)

    def col_peer(k):
        return 2 * peer(m, k) + core

    def fetch(i, src, dst):
        return pltpu.make_async_copy(src, dst, fetch_sem.at[i])

    fetch_x = fetch(0, x_hbm, current.at[0])
    fetch_row = fetch(1, trow_hbm, trow_ref)
    fetch_col = fetch(2, tcol_hbm, tcol_ref)
    fetch_tiles = fetch(3, tiles_hbm, tiles)
    fetch_x.start()

    barrier = pltpu.get_barrier_semaphore()

    @functools.partial(loop, peers, unroll=True)
    def _(k):
        pl.semaphore_signal(barrier, inc=1, device_id=(r, row_peer(k)), device_id_type=MESH)
        pl.semaphore_signal(barrier, inc=1, device_id=(col_peer(k), c), device_id_type=MESH)

    pl.semaphore_signal(barrier, inc=1, device_id=(partner, c), device_id_type=MESH)
    fetch_row.start()
    fetch_col.start()
    fetch_tiles.start()
    fetch_x.wait()
    pl.semaphore_wait(barrier, 2 * peers + 1)

    def remote(src, dst, send, recv, row, col):
        return pltpu.make_async_remote_copy(
            src_ref=src, dst_ref=dst, send_sem=send, recv_sem=recv, device_id=(row, col), device_id_type=MESH
        )

    def rows_of(h):
        return pl.ds(pl.multiple_of(h * height, height), height)

    def gather_row(a, h, k):
        src = current.at[a, rows_of(h)]
        return remote(src, rowx.at[a, h, k], send_gr.at[a, h, k], recv_gr.at[a, h, k], r, row_peer(k))

    def gather_col(a, h, k):
        src = current.at[a, rows_of(h)]
        dst = colx.at[a, h, core * chips + k]
        return remote(src, dst, send_gc.at[a, h, k], recv_gc.at[a, h, k], col_peer(k), c)

    def forward(a, h, j):
        blocks = colx.at[a, h, pl.ds(core * chips + j * BATCH, BATCH)]
        return remote(blocks, blocks, send_fw.at[a, h, j], recv_fw.at[a, h, j], partner, c)

    def swap(a, h, j):
        half = pl.ds(j * (chips // 2), chips // 2)
        return remote(
            swap_out.at[a, h, half], swap_in.at[a, h, half], send_sw.at[a, h, j], recv_sw.at[a, h, j], partner, c
        )

    def scatter_col(a, h, k):
        return remote(
            out_c.at[a, h, k], in_c.at[a, h, k], send_sc.at[a, h, k], recv_sc.at[a, h, k], col_peer(k), c
        )

    def scatter_row(a, h, k):
        return remote(
            out_r.at[a, h, k], in_r.at[a, h, k], send_sr.at[a, h, k], recv_sr.at[a, h, k], r, row_peer(k)
        )

    def trow(s):
        return trow_ref[0, s]

    def tcol(s):
        return tcol_ref[0, s]

    def tables():
        part_c[zero_slot] = jnp.zeros(part_c.shape[1:], part_c.dtype)
        part_r[zero_slot] = jnp.zeros(part_r.shape[1:], part_r.dtype)

        @functools.partial(loop, n_col)
        def _(k):
            p = peer(c, k)
            one = jnp.int32(0)
            for s in range(n_col):
                one = jnp.where(trow(s) == p, s, one)
            two = jnp.int32(zero_slot)
            for s in range(n_col, slots):
                two = jnp.where(trow(s) == p, s, two)
            row_slot[k] = one
            row_extra[k] = two

        @functools.partial(loop, chips)
        def _(k):
            q = 2 * peer(m, k) + core
            mine, other = jnp.int32(zero_slot), jnp.int32(zero_slot)
            for s in range(slots):
                mine = jnp.where(tcol(s) == q, s, mine)
                other = jnp.where(tcol(s) == q + 1 - 2 * core, s, other)
            own_last[k] = mine
            other_last[k] = other

        @functools.partial(loop, chips)
        def _(k):
            place_of_chip[source(m, k)] = k
            row_place[source(c, k)] = k

        @functools.partial(loop, slots)
        def _(s):
            here = jnp.int32(zero_slot)
            for t in range(slots):
                here = jnp.where((tcol(t) == tcol(s)) & (t < s), t, here)
            prev_slot[s] = here
            left_row[s] = row_place[jnp.maximum(trow(s), 0)]
            q = jnp.maximum(tcol(s), 0)
            col_place[s] = lax.rem(q, 2) * chips + place_of_chip[lax.div(q, 2)]

    def start_gather(a, h):
        @functools.partial(loop, peers, unroll=True)
        def _(k):
            gather_row(a, h, k).start()
            gather_col(a, h, k).start()

        block = current[a, rows_of(h)]
        rowx[a, h, n_col - 1] = block
        colx[a, h, core * chips + chips - 1] = block

    def products(a, h):
        scale = jnp.where(a == 0, SCALES[0], SCALES[1])

        for j in range(chips // BATCH):
            for k in range(j * BATCH, min((j + 1) * BATCH, peers)):
                gather_col(a, h, k).wait_recv()
            forward(a, h, j).start()
        for k in range(peers):
            gather_row(a, h, k).wait_recv()

        for k in range(n_col):
            row_now[k] = rowx[a, h, k]
        for s in range(slots):
            part_c[s] = jnp.dot(row_now[left_row[s]], tiles[s], preferred_element_type=jnp.float32)
        for s in range(slots):
            part_c[s] = part_c[s] + part_c[prev_slot[s]]

        for j in range(2):
            for k in range(j * (chips // 2), (j + 1) * (chips // 2)):
                swap_out[a, h, k] = part_c[other_last[k]]
            swap(a, h, j).start()
        for j in range(chips // BATCH):
            forward(a, h, j).wait_recv()

        for k in range(n_row):
            col_now[k] = colx[a, h, k]
        for s in range(slots):
            part_r[s] = lax.dot_general(
                col_now[col_place[s]], tiles[s], (((1,), (1,)), ((), ())), preferred_element_type=jnp.float32
            )

        def row_sum(k):
            return part_r[row_slot[k]] + part_r[row_extra[k]]

        def col_sum(k):
            return part_c[own_last[k]] + swap_in[a, h, k]

        def send(sums, out, copy):
            for g in range(0, peers, GROUP):
                for k in range(g, g + GROUP):
                    out[a, h, k] = encode(sums(k), scale)
                for k in range(g, g + GROUP):
                    copy(a, h, k).start()

        send(row_sum, out_r, scatter_row)
        swap(a, h, 0).wait_recv()
        swap(a, h, 1).wait_recv()
        send(col_sum, out_c, scatter_col)
        own[h] = row_sum(n_col - 1) + col_sum(chips - 1)

    def collect(a, h):
        scale = jnp.where(a == 0, 1.0 / SCALES[0], 1.0 / SCALES[1])

        total = own[h]
        for g in range(0, peers, GROUP):
            for k in range(g, g + GROUP):
                scatter_row(a, h, k).wait_recv()
                scatter_col(a, h, k).wait_recv()
            for k in range(g, g + GROUP):
                total = total + (decode(in_r[a, h, k], scale) + decode(in_c[a, h, k], scale))
        return total

    def drain():
        @functools.partial(loop, 2)
        def _(a):
            @functools.partial(loop, PARTS)
            def _(h):
                @functools.partial(loop, 2)
                def _(j):
                    swap(a, h, j).wait_send()

                @functools.partial(loop, chips // BATCH)
                def _(j):
                    forward(a, h, j).wait_send()

                @functools.partial(loop, peers, unroll=5)
                def _(k):
                    gather_row(a, h, k).wait_send()
                    gather_col(a, h, k).wait_send()
                    scatter_row(a, h, k).wait_send()
                    scatter_col(a, h, k).wait_send()

    @functools.partial(loop, 3)
    def _(a):
        @pl.when(a == 2)
        def _():
            drain()

        @functools.partial(loop, PARTS)
        def _(h):
            @pl.when(a > 0)
            def _():
                total = collect(a - 1, h)
                before = current[a - 1, rows_of(h)].astype(jnp.float32)

                @pl.when(a == 1)
                def _():
                    first = ((total - CENTER * before) / HALF_WIDTH).astype(jnp.bfloat16)
                    current[1, rows_of(h)] = first
                    first_ref[rows_of(h)] = first

                @pl.when(a == 2)
                def _():
                    x = current[0, rows_of(h)].astype(jnp.float32)
                    second_ref[rows_of(h)] = 2.0 * (total - CENTER * before) / HALF_WIDTH - x

            @pl.when(a < 2)
            def _():
                start_gather(a, h)

        @pl.when(a == 0)
        def _():
            fetch_row.wait()
            fetch_col.wait()
            tables()
            fetch_tiles.wait()

        @pl.when(a < 2)
        def _():
            @functools.partial(loop, PARTS)
            def _(h):
                products(a, h)


def shards(vectors, tiles, tile_row, tile_col):
    n_row = lax.axis_size("row")
    n_col = lax.axis_size("col")
    slots = tiles.shape[2]
    block = tiles.shape[-1]
    count = vectors.shape[0]
    chips = n_row // 2
    height = count // PARTS
    f32, bf16, i16 = jnp.float32, jnp.bfloat16, jnp.int16
    dma = pltpu.SemaphoreType.DMA
    vmem = pl.BlockSpec(memory_space=pltpu.VMEM)
    hbm = pl.BlockSpec(memory_space=pltpu.HBM)
    return pl.pallas_call(
        functools.partial(filter_kernel, n_row, n_col, slots),
        out_shape=(
            jax.ShapeDtypeStruct((count, block), bf16),
            jax.ShapeDtypeStruct((count, block), f32),
        ),
        in_specs=[hbm] * 4,
        out_specs=(vmem, vmem),
        scratch_shapes=[
            pltpu.SMEM((1, slots), jnp.int32),
            pltpu.SMEM((1, slots), jnp.int32),
            pltpu.VMEM((slots, block, block), bf16),
            pltpu.VMEM((2, count, block), bf16),
            pltpu.VMEM((PARTS, height, block), f32),
            pltpu.VMEM((n_col, height, block), bf16),
            pltpu.VMEM((n_row, height, block), bf16),
            pltpu.VMEM((2, PARTS, n_col, height, block), bf16),
            pltpu.VMEM((2, PARTS, n_row, height, block), bf16),
            pltpu.VMEM((slots + 1, height, block), f32),
            pltpu.VMEM((slots + 1, height, block), f32),
            pltpu.VMEM((2, PARTS, chips, height, block), f32),
            pltpu.VMEM((2, PARTS, chips, height, block), f32),
        ]
        + [pltpu.VMEM((2, PARTS, chips, height, block), i16)] * 4
        + [
            pltpu.SMEM((n_col,), jnp.int32),
            pltpu.SMEM((n_col,), jnp.int32),
            pltpu.SMEM((slots,), jnp.int32),
            pltpu.SMEM((chips,), jnp.int32),
            pltpu.SMEM((chips,), jnp.int32),
            pltpu.SMEM((chips,), jnp.int32),
            pltpu.SMEM((n_col,), jnp.int32),
            pltpu.SMEM((slots,), jnp.int32),
            pltpu.SMEM((slots,), jnp.int32),
            dma((4,)),
        ]
        + [dma((2, PARTS, n_col))] * 8
        + [dma((2, PARTS, chips // BATCH))] * 2
        + [dma((2, PARTS, 2))] * 2,
        compiler_params=pltpu.CompilerParams(
            collective_id=0, has_side_effects=True, vmem_limit_bytes=64 * 1024 * 1024 - 600 * 1024
        ),
        cost_estimate=pl.CostEstimate(
            flops=8 * slots * count * block * block, bytes_accessed=2 * slots * block * block, transcendentals=0
        ),
    )(tile_row[0], tile_col[0], vectors, tiles[0, 0])


def solution(mesh):
    placed = (
        P(None, ("row", "col")),
        P("row", "col", None, None, None),
        P("row", "col", None),
        P("row", "col", None),
    )
    return jax.shard_map(
        shards,
        mesh=mesh,
        in_specs=placed,
        out_specs=(P(None, ("row", "col")), P(None, ("row", "col"))),
        check_vma=False,
    )
```

```python
import functools

import jax
import jax.numpy as jnp
from jax import lax
from jax.experimental import pallas as pl
from jax.experimental.pallas import tpu as pltpu
from jax.sharding import PartitionSpec as P

CENTER = 0.5
HALF_WIDTH = 1.5
MESH = pl.DeviceIdType.MESH
BATCH = 4
PARTS = 2

LIMITS = (2.0**12, 2.0**24)
SCALES = tuple(32767.0 / limit ** (1 / 16) for limit in LIMITS)
TINY = 1e-30
GROUP = 3


def encode(v, scale):
    root = lax.rsqrt(lax.rsqrt(lax.rsqrt(lax.rsqrt(jnp.maximum(jnp.abs(v), TINY)))))
    code = jnp.where(jnp.abs(v) <= TINY, 0.0, root * scale + 0.5)
    return jnp.where(v < 0, -code, code).astype(jnp.int32).astype(jnp.int16)


def decode(code, scale):
    code = code.astype(jnp.int32).astype(jnp.float32)
    power = code * scale
    power = power * power
    power = power * power
    power = power * power
    power = power * power
    return jnp.where(code < 0, -power, power)


def filter_kernel(n_row, n_col, slots, trow_hbm, tcol_hbm, x_hbm, tiles_hbm, first_ref, second_ref, *scratch):
    (
        trow_ref, tcol_ref, tiles, current, own, row_now, col_now, rowx, colx, part_c, part_r, swap_out, swap_in,
        out_c, out_r, in_c, in_r, row_slot, row_extra, prev_slot, own_last, other_last, place_of_chip, row_place,
        left_row, col_place,
        fetch_sem, send_gr, recv_gr, send_gc, recv_gc, send_sc, recv_sc, send_sr, recv_sr,
        send_fw, recv_fw, send_sw, recv_sw,
    ) = scratch
    r = lax.axis_index("row")
    c = lax.axis_index("col")
    chips = n_row // 2
    assert chips == n_col
    ring = n_col // 2
    m = r // 2
    core = r - 2 * m
    partner = r + 1 - 2 * core
    zero_slot = slots
    height = current.shape[1] // PARTS
    peers = n_col - 1

    def loop(count, body, unroll=1):
        def step(k, _):
            body(k)
            return 0

        lax.fori_loop(0, count, step, 0, unroll=unroll)

    def offset(k):
        i = k // 2
        j = (i + 1) // 2
        return ring // 2 + j * (1 - 2 * (i % 2)), 1 - k % 2

    def peer(index, k):
        d, x = offset(k)
        return 2 * lax.rem(index // 2 + d, ring) + lax.rem(index % 2 + x, 2)

    def source(index, k):
        d, x = offset(k)
        return 2 * lax.rem(index // 2 + ring - d, ring) + lax.rem(index % 2 + x, 2)

    def row_peer(k):
        return peer(c, k)

    def col_peer(k):
        return 2 * peer(m, k) + core

    def fetch(i, src, dst):
        return pltpu.make_async_copy(src, dst, fetch_sem.at[i])

    fetch_x = fetch(0, x_hbm, current.at[0])
    fetch_row = fetch(1, trow_hbm, trow_ref)
    fetch_col = fetch(2, tcol_hbm, tcol_ref)
    fetch_tiles = fetch(3, tiles_hbm, tiles)
    fetch_x.start()

    barrier = pltpu.get_barrier_semaphore()

    @functools.partial(loop, peers, unroll=True)
    def _(k):
        pl.semaphore_signal(barrier, inc=1, device_id=(r, row_peer(k)), device_id_type=MESH)
        pl.semaphore_signal(barrier, inc=1, device_id=(col_peer(k), c), device_id_type=MESH)

    pl.semaphore_signal(barrier, inc=1, device_id=(partner, c), device_id_type=MESH)
    fetch_row.start()
    fetch_col.start()
    fetch_tiles.start()
    fetch_x.wait()
    pl.semaphore_wait(barrier, 2 * peers + 1)

    def remote(src, dst, send, recv, row, col):
        return pltpu.make_async_remote_copy(
            src_ref=src, dst_ref=dst, send_sem=send, recv_sem=recv, device_id=(row, col), device_id_type=MESH
        )

    def rows_of(h):
        return pl.ds(pl.multiple_of(h * height, height), height)

    def gather_row(a, h, k):
        src = current.at[a, rows_of(h)]
        return remote(src, rowx.at[a, h, k], send_gr.at[a, h, k], recv_gr.at[a, h, k], r, row_peer(k))

    def gather_col(a, h, k):
        src = current.at[a, rows_of(h)]
        dst = colx.at[a, h, core * chips + k]
        return remote(src, dst, send_gc.at[a, h, k], recv_gc.at[a, h, k], col_peer(k), c)

    def forward(a, h, j):
        blocks = colx.at[a, h, pl.ds(core * chips + j * BATCH, BATCH)]
        return remote(blocks, blocks, send_fw.at[a, h, j], recv_fw.at[a, h, j], partner, c)

    def swap(a, h, j):
        half = pl.ds(j * (chips // 2), chips // 2)
        return remote(
            swap_out.at[a, h, half], swap_in.at[a, h, half], send_sw.at[a, h, j], recv_sw.at[a, h, j], partner, c
        )

    def scatter_col(a, h, k):
        return remote(
            out_c.at[a, h, k], in_c.at[a, h, k], send_sc.at[a, h, k], recv_sc.at[a, h, k], col_peer(k), c
        )

    def scatter_row(a, h, k):
        return remote(
            out_r.at[a, h, k], in_r.at[a, h, k], send_sr.at[a, h, k], recv_sr.at[a, h, k], r, row_peer(k)
        )

    def trow(s):
        return trow_ref[0, s]

    def tcol(s):
        return tcol_ref[0, s]

    def tables():
        part_c[zero_slot] = jnp.zeros(part_c.shape[1:], part_c.dtype)
        part_r[zero_slot] = jnp.zeros(part_r.shape[1:], part_r.dtype)

        @functools.partial(loop, n_col)
        def _(k):
            p = peer(c, k)
            one = jnp.int32(0)
            for s in range(n_col):
                one = jnp.where(trow(s) == p, s, one)
            two = jnp.int32(zero_slot)
            for s in range(n_col, slots):
                two = jnp.where(trow(s) == p, s, two)
            row_slot[k] = one
            row_extra[k] = two

        @functools.partial(loop, chips)
        def _(k):
            q = 2 * peer(m, k) + core
            mine, other = jnp.int32(zero_slot), jnp.int32(zero_slot)
            for s in range(slots):
                mine = jnp.where(tcol(s) == q, s, mine)
                other = jnp.where(tcol(s) == q + 1 - 2 * core, s, other)
            own_last[k] = mine
            other_last[k] = other

        @functools.partial(loop, chips)
        def _(k):
            place_of_chip[source(m, k)] = k
            row_place[source(c, k)] = k

        @functools.partial(loop, slots)
        def _(s):
            here = jnp.int32(zero_slot)
            for t in range(slots):
                here = jnp.where((tcol(t) == tcol(s)) & (t < s), t, here)
            prev_slot[s] = here
            left_row[s] = row_place[jnp.maximum(trow(s), 0)]
            q = jnp.maximum(tcol(s), 0)
            col_place[s] = lax.rem(q, 2) * chips + place_of_chip[lax.div(q, 2)]

    def start_gather(a, h):
        @functools.partial(loop, peers, unroll=True)
        def _(k):
            gather_row(a, h, k).start()
            gather_col(a, h, k).start()

        block = current[a, rows_of(h)]
        rowx[a, h, n_col - 1] = block
        colx[a, h, core * chips + chips - 1] = block

    def products(a, h):
        scale = jnp.where(a == 0, SCALES[0], SCALES[1])

        for j in range(chips // BATCH):
            for k in range(j * BATCH, min((j + 1) * BATCH, peers)):
                gather_col(a, h, k).wait_recv()
            forward(a, h, j).start()
        for k in range(peers):
            gather_row(a, h, k).wait_recv()

        for k in range(n_col):
            row_now[k] = rowx[a, h, k]
        for s in range(slots):
            part_c[s] = jnp.dot(row_now[left_row[s]], tiles[s], preferred_element_type=jnp.float32)
        for s in range(slots):
            part_c[s] = part_c[s] + part_c[prev_slot[s]]

        for j in range(2):
            for k in range(j * (chips // 2), (j + 1) * (chips // 2)):
                swap_out[a, h, k] = part_c[other_last[k]]
            swap(a, h, j).start()
        for j in range(chips // BATCH):
            forward(a, h, j).wait_recv()

        for k in range(n_row):
            col_now[k] = colx[a, h, k]
        for s in range(slots):
            part_r[s] = lax.dot_general(
                col_now[col_place[s]], tiles[s], (((1,), (1,)), ((), ())), preferred_element_type=jnp.float32
            )

        def row_sum(k):
            return part_r[row_slot[k]] + part_r[row_extra[k]]

        def col_sum(k):
            return part_c[own_last[k]] + swap_in[a, h, k]

        def send(sums, out, copy):
            for g in range(0, peers, GROUP):
                for k in range(g, g + GROUP):
                    out[a, h, k] = encode(sums(k), scale)
                for k in range(g, g + GROUP):
                    copy(a, h, k).start()

        send(row_sum, out_r, scatter_row)
        swap(a, h, 0).wait_recv()
        swap(a, h, 1).wait_recv()
        send(col_sum, out_c, scatter_col)
        own[h] = row_sum(n_col - 1) + col_sum(chips - 1)

    def collect(a, h):
        scale = jnp.where(a == 0, 1.0 / SCALES[0], 1.0 / SCALES[1])

        total = own[h]
        for g in range(0, peers, GROUP):
            for k in range(g, g + GROUP):
                scatter_row(a, h, k).wait_recv()
                scatter_col(a, h, k).wait_recv()
            for k in range(g, g + GROUP):
                total = total + (decode(in_r[a, h, k], scale) + decode(in_c[a, h, k], scale))
        return total

    def drain():
        @functools.partial(loop, 2)
        def _(a):
            @functools.partial(loop, PARTS)
            def _(h):
                @functools.partial(loop, 2)
                def _(j):
                    swap(a, h, j).wait_send()

                @functools.partial(loop, chips // BATCH)
                def _(j):
                    forward(a, h, j).wait_send()

                @functools.partial(loop, peers, unroll=5)
                def _(k):
                    gather_row(a, h, k).wait_send()
                    gather_col(a, h, k).wait_send()
                    scatter_row(a, h, k).wait_send()
                    scatter_col(a, h, k).wait_send()

    @functools.partial(loop, 3)
    def _(a):
        @pl.when(a == 2)
        def _():
            drain()

        @functools.partial(loop, PARTS)
        def _(h):
            @pl.when(a > 0)
            def _():
                total = collect(a - 1, h)
                before = current[a - 1, rows_of(h)].astype(jnp.float32)

                @pl.when(a == 1)
                def _():
                    first = ((total - CENTER * before) / HALF_WIDTH).astype(jnp.bfloat16)
                    current[1, rows_of(h)] = first
                    first_ref[rows_of(h)] = first

                @pl.when(a == 2)
                def _():
                    x = current[0, rows_of(h)].astype(jnp.float32)
                    second_ref[rows_of(h)] = 2.0 * (total - CENTER * before) / HALF_WIDTH - x

            @pl.when(a < 2)
            def _():
                start_gather(a, h)

        @pl.when(a == 0)
        def _():
            fetch_row.wait()
            fetch_col.wait()
            tables()
            fetch_tiles.wait()

        @pl.when(a < 2)
        def _():
            @functools.partial(loop, PARTS)
            def _(h):
                products(a, h)


def shards(vectors, tiles, tile_row, tile_col):
    n_row = lax.axis_size("row")
    n_col = lax.axis_size("col")
    slots = tiles.shape[2]
    block = tiles.shape[-1]
    count = vectors.shape[0]
    chips = n_row // 2
    height = count // PARTS
    f32, bf16, i16 = jnp.float32, jnp.bfloat16, jnp.int16
    dma = pltpu.SemaphoreType.DMA
    vmem = pl.BlockSpec(memory_space=pltpu.VMEM)
    hbm = pl.BlockSpec(memory_space=pltpu.HBM)
    return pl.pallas_call(
        functools.partial(filter_kernel, n_row, n_col, slots),
        out_shape=(
            pltpu.VMEM((count, block), bf16),
            pltpu.VMEM((count, block), f32),
        ),
        in_specs=[hbm] * 4,
        out_specs=(vmem, vmem),
        scratch_shapes=[
            pltpu.SMEM((1, slots), jnp.int32),
            pltpu.SMEM((1, slots), jnp.int32),
            pltpu.VMEM((slots, block, block), bf16),
            pltpu.VMEM((2, count, block), bf16),
            pltpu.VMEM((PARTS, height, block), f32),
            pltpu.VMEM((n_col, height, block), bf16),
            pltpu.VMEM((n_row, height, block), bf16),
            pltpu.VMEM((2, PARTS, n_col, height, block), bf16),
            pltpu.VMEM((2, PARTS, n_row, height, block), bf16),
            pltpu.VMEM((slots + 1, height, block), f32),
            pltpu.VMEM((slots + 1, height, block), f32),
            pltpu.VMEM((2, PARTS, chips, height, block), f32),
            pltpu.VMEM((2, PARTS, chips, height, block), f32),
        ]
        + [pltpu.VMEM((2, PARTS, chips, height, block), i16)] * 4
        + [
            pltpu.SMEM((n_col,), jnp.int32),
            pltpu.SMEM((n_col,), jnp.int32),
            pltpu.SMEM((slots,), jnp.int32),
            pltpu.SMEM((chips,), jnp.int32),
            pltpu.SMEM((chips,), jnp.int32),
            pltpu.SMEM((chips,), jnp.int32),
            pltpu.SMEM((n_col,), jnp.int32),
            pltpu.SMEM((slots,), jnp.int32),
            pltpu.SMEM((slots,), jnp.int32),
            dma((4,)),
        ]
        + [dma((2, PARTS, n_col))] * 8
        + [dma((2, PARTS, chips // BATCH))] * 2
        + [dma((2, PARTS, 2))] * 2,
        compiler_params=pltpu.CompilerParams(
            collective_id=0, has_side_effects=True, vmem_limit_bytes=60 * 1024 * 1024
        ),
        cost_estimate=pl.CostEstimate(
            flops=8 * slots * count * block * block, bytes_accessed=2 * slots * block * block, transcendentals=0
        ),
    )(tile_row[0], tile_col[0], vectors, tiles[0, 0])


def solution(mesh):
    placed = (
        P(None, ("row", "col")),
        P("row", "col", None, None, None),
        P("row", "col", None),
        P("row", "col", None),
    )
    return jax.shard_map(
        shards,
        mesh=mesh,
        in_specs=placed,
        out_specs=(P(None, ("row", "col")), P(None, ("row", "col"))),
        check_vma=False,
    )
```

```python
import functools

import jax
import jax.numpy as jnp
from jax import lax
from jax.experimental import pallas as pl
from jax.experimental.pallas import tpu as pltpu
from jax.sharding import PartitionSpec as P

CENTER = 0.5
HALF_WIDTH = 1.5
MESH = pl.DeviceIdType.MESH
BATCH = 4
PARTS = 2

LIMITS = (2.0**12, 2.0**24)
SCALES = tuple(32767.0 / limit ** (1 / 16) for limit in LIMITS)
TINY = 1e-30
GROUP = 3


def encode(v, scale):
    root = lax.rsqrt(lax.rsqrt(lax.rsqrt(lax.rsqrt(jnp.maximum(jnp.abs(v), TINY)))))
    code = jnp.where(jnp.abs(v) <= TINY, 0.0, root * scale + 0.5)
    return jnp.where(v < 0, -code, code).astype(jnp.int32).astype(jnp.int16)


def decode(code, scale):
    code = code.astype(jnp.int32).astype(jnp.float32)
    power = code * scale
    power = power * power
    power = power * power
    power = power * power
    power = power * power
    return jnp.where(code < 0, -power, power)


def filter_kernel(n_row, n_col, slots, trow_hbm, tcol_hbm, x_hbm, tiles_hbm, first_ref, second_ref, *scratch):
    (
        trow_ref, tcol_ref, tiles, current, own, row_now, col_now, rowx, colx, part_c, part_r, swap_out, swap_in,
        out_c, out_r, in_c, in_r, row_slot, row_extra, prev_slot, own_last, other_last, place_of_chip, row_place,
        left_row, col_place,
        fetch_sem, send_gr, recv_gr, send_gc, recv_gc, send_sc, recv_sc, send_sr, recv_sr,
        send_fw, recv_fw, send_sw, recv_sw,
    ) = scratch
    r = lax.axis_index("row")
    c = lax.axis_index("col")
    chips = n_row // 2
    assert chips == n_col
    ring = n_col // 2
    m = r // 2
    core = r - 2 * m
    partner = r + 1 - 2 * core
    zero_slot = slots
    height = current.shape[1] // PARTS
    peers = n_col - 1

    def loop(count, body, unroll=1):
        def step(k, _):
            body(k)
            return 0

        lax.fori_loop(0, count, step, 0, unroll=unroll)

    def offset(k):
        i = k // 2
        j = (i + 1) // 2
        return ring // 2 + j * (1 - 2 * (i % 2)), 1 - k % 2

    def peer(index, k):
        d, x = offset(k)
        return 2 * lax.rem(index // 2 + d, ring) + lax.rem(index % 2 + x, 2)

    def source(index, k):
        d, x = offset(k)
        return 2 * lax.rem(index // 2 + ring - d, ring) + lax.rem(index % 2 + x, 2)

    def row_peer(k):
        return peer(c, k)

    def col_peer(k):
        return 2 * peer(m, k) + core

    def fetch(i, src, dst):
        return pltpu.make_async_copy(src, dst, fetch_sem.at[i])

    fetch_x = fetch(0, x_hbm, current.at[0])
    fetch_row = fetch(1, trow_hbm, trow_ref)
    fetch_col = fetch(2, tcol_hbm, tcol_ref)
    fetch_tiles = fetch(3, tiles_hbm, tiles)
    fetch_x.start()

    barrier = pltpu.get_barrier_semaphore()

    @functools.partial(loop, peers, unroll=True)
    def _(k):
        pl.semaphore_signal(barrier, inc=1, device_id=(r, row_peer(k)), device_id_type=MESH)
        pl.semaphore_signal(barrier, inc=1, device_id=(col_peer(k), c), device_id_type=MESH)

    pl.semaphore_signal(barrier, inc=1, device_id=(partner, c), device_id_type=MESH)
    fetch_row.start()
    fetch_col.start()
    fetch_tiles.start()
    fetch_x.wait()
    pl.semaphore_wait(barrier, 2 * peers + 1)

    def remote(src, dst, send, recv, row, col):
        return pltpu.make_async_remote_copy(
            src_ref=src, dst_ref=dst, send_sem=send, recv_sem=recv, device_id=(row, col), device_id_type=MESH
        )

    def rows_of(h):
        return pl.ds(pl.multiple_of(h * height, height), height)

    def gather_row(a, h, k):
        src = current.at[a, rows_of(h)]
        return remote(src, rowx.at[a, h, k], send_gr.at[a, h, k], recv_gr.at[a, h, k], r, row_peer(k))

    def gather_col(a, h, k):
        src = current.at[a, rows_of(h)]
        dst = colx.at[a, h, core * chips + k]
        return remote(src, dst, send_gc.at[a, h, k], recv_gc.at[a, h, k], col_peer(k), c)

    def forward(a, h, j):
        blocks = colx.at[a, h, pl.ds(core * chips + j * BATCH, BATCH)]
        return remote(blocks, blocks, send_fw.at[a, h, j], recv_fw.at[a, h, j], partner, c)

    def swap(a, h, j):
        half = pl.ds(j * (chips // 2), chips // 2)
        return remote(
            swap_out.at[a, h, half], swap_in.at[a, h, half], send_sw.at[a, h, j], recv_sw.at[a, h, j], partner, c
        )

    def scatter_col(a, h, k):
        return remote(
            out_c.at[a, h, k], in_c.at[a, h, k], send_sc.at[a, h, k], recv_sc.at[a, h, k], col_peer(k), c
        )

    def scatter_row(a, h, k):
        return remote(
            out_r.at[a, h, k], in_r.at[a, h, k], send_sr.at[a, h, k], recv_sr.at[a, h, k], r, row_peer(k)
        )

    def trow(s):
        return trow_ref[0, s]

    def tcol(s):
        return tcol_ref[0, s]

    def tables():
        part_c[zero_slot] = jnp.zeros(part_c.shape[1:], part_c.dtype)
        part_r[zero_slot] = jnp.zeros(part_r.shape[1:], part_r.dtype)

        @functools.partial(loop, n_col)
        def _(k):
            p = peer(c, k)
            one = jnp.int32(0)
            for s in range(n_col):
                one = jnp.where(trow(s) == p, s, one)
            two = jnp.int32(zero_slot)
            for s in range(n_col, slots):
                two = jnp.where(trow(s) == p, s, two)
            row_slot[k] = one
            row_extra[k] = two

        @functools.partial(loop, chips)
        def _(k):
            q = 2 * peer(m, k) + core
            mine, other = jnp.int32(zero_slot), jnp.int32(zero_slot)
            for s in range(slots):
                mine = jnp.where(tcol(s) == q, s, mine)
                other = jnp.where(tcol(s) == q + 1 - 2 * core, s, other)
            own_last[k] = mine
            other_last[k] = other

        @functools.partial(loop, chips)
        def _(k):
            place_of_chip[source(m, k)] = k
            row_place[source(c, k)] = k

        @functools.partial(loop, slots)
        def _(s):
            here = jnp.int32(zero_slot)
            for t in range(slots):
                here = jnp.where((tcol(t) == tcol(s)) & (t < s), t, here)
            prev_slot[s] = here
            left_row[s] = row_place[jnp.maximum(trow(s), 0)]
            q = jnp.maximum(tcol(s), 0)
            col_place[s] = lax.rem(q, 2) * chips + place_of_chip[lax.div(q, 2)]

    def start_gather(a, h):
        @functools.partial(loop, peers, unroll=True)
        def _(k):
            gather_row(a, h, k).start()
            gather_col(a, h, k).start()

        block = current[a, rows_of(h)]
        rowx[a, h, n_col - 1] = block
        colx[a, h, core * chips + chips - 1] = block

    def products(a, h):
        scale = jnp.where(a == 0, SCALES[0], SCALES[1])

        for j in range(chips // BATCH):
            for k in range(j * BATCH, min((j + 1) * BATCH, peers)):
                gather_col(a, h, k).wait_recv()
            forward(a, h, j).start()
        for k in range(peers):
            gather_row(a, h, k).wait_recv()

        for k in range(n_col):
            row_now[k] = rowx[a, h, k]
        for s in range(slots):
            part_c[s] = jnp.dot(row_now[left_row[s]], tiles[s], preferred_element_type=jnp.float32)
        for s in range(slots):
            part_c[s] = part_c[s] + part_c[prev_slot[s]]

        for j in range(2):
            for k in range(j * (chips // 2), (j + 1) * (chips // 2)):
                swap_out[a, h, k] = part_c[other_last[k]]
            swap(a, h, j).start()
        for k in range(chips):
            col_now[core * chips + k] = colx[a, h, core * chips + k]
        for j in range(chips // BATCH):
            forward(a, h, j).wait_recv()

        for k in range(chips):
            col_now[(1 - core) * chips + k] = colx[a, h, (1 - core) * chips + k]
        for s in range(slots):
            part_r[s] = lax.dot_general(
                col_now[col_place[s]], tiles[s], (((1,), (1,)), ((), ())), preferred_element_type=jnp.float32
            )

        def row_sum(k):
            return part_r[row_slot[k]] + part_r[row_extra[k]]

        def col_sum(k):
            return part_c[own_last[k]] + swap_in[a, h, k]

        def send(sums, out, copy, swapped):
            for g in range(0, peers, GROUP):
                if swapped and g == 0:
                    swap(a, h, 0).wait_recv()
                if swapped and g < chips // 2 <= g + GROUP:
                    swap(a, h, 1).wait_recv()
                for k in range(g, g + GROUP):
                    out[a, h, k] = encode(sums(k), scale)
                for k in range(g, g + GROUP):
                    copy(a, h, k).start()

        send(row_sum, out_r, scatter_row, False)
        send(col_sum, out_c, scatter_col, True)
        own[h] = row_sum(n_col - 1) + col_sum(chips - 1)

    def collect(a, h):
        scale = jnp.where(a == 0, 1.0 / SCALES[0], 1.0 / SCALES[1])

        total = own[h]
        for g in range(0, peers, GROUP):
            for k in range(g, g + GROUP):
                scatter_row(a, h, k).wait_recv()
                scatter_col(a, h, k).wait_recv()
            for k in range(g, g + GROUP):
                total = total + (decode(in_r[a, h, k], scale) + decode(in_c[a, h, k], scale))
        return total

    def drain():
        @functools.partial(loop, 2)
        def _(a):
            @functools.partial(loop, PARTS)
            def _(h):
                @functools.partial(loop, 2)
                def _(j):
                    swap(a, h, j).wait_send()

                @functools.partial(loop, chips // BATCH)
                def _(j):
                    forward(a, h, j).wait_send()

                @functools.partial(loop, peers, unroll=5)
                def _(k):
                    gather_row(a, h, k).wait_send()
                    gather_col(a, h, k).wait_send()
                    scatter_row(a, h, k).wait_send()
                    scatter_col(a, h, k).wait_send()

    @functools.partial(loop, 3)
    def _(a):
        @pl.when(a == 2)
        def _():
            drain()

        @functools.partial(loop, PARTS)
        def _(h):
            @pl.when(a > 0)
            def _():
                total = collect(a - 1, h)
                before = current[a - 1, rows_of(h)].astype(jnp.float32)

                @pl.when(a == 1)
                def _():
                    first = ((total - CENTER * before) / HALF_WIDTH).astype(jnp.bfloat16)
                    current[1, rows_of(h)] = first
                    first_ref[rows_of(h)] = first

                @pl.when(a == 2)
                def _():
                    x = current[0, rows_of(h)].astype(jnp.float32)
                    second_ref[rows_of(h)] = 2.0 * (total - CENTER * before) / HALF_WIDTH - x

            @pl.when(a < 2)
            def _():
                start_gather(a, h)

        @pl.when(a == 0)
        def _():
            fetch_row.wait()
            fetch_col.wait()
            tables()
            fetch_tiles.wait()

        @pl.when(a < 2)
        def _():
            @functools.partial(loop, PARTS)
            def _(h):
                products(a, h)


def shards(vectors, tiles, tile_row, tile_col):
    n_row = lax.axis_size("row")
    n_col = lax.axis_size("col")
    slots = tiles.shape[2]
    block = tiles.shape[-1]
    count = vectors.shape[0]
    chips = n_row // 2
    height = count // PARTS
    f32, bf16, i16 = jnp.float32, jnp.bfloat16, jnp.int16
    dma = pltpu.SemaphoreType.DMA
    vmem = pl.BlockSpec(memory_space=pltpu.VMEM)
    hbm = pl.BlockSpec(memory_space=pltpu.HBM)
    return pl.pallas_call(
        functools.partial(filter_kernel, n_row, n_col, slots),
        out_shape=(
            pltpu.VMEM((count, block), bf16),
            pltpu.VMEM((count, block), f32),
        ),
        in_specs=[hbm] * 4,
        out_specs=(vmem, vmem),
        scratch_shapes=[
            pltpu.SMEM((1, slots), jnp.int32),
            pltpu.SMEM((1, slots), jnp.int32),
            pltpu.VMEM((slots, block, block), bf16),
            pltpu.VMEM((2, count, block), bf16),
            pltpu.VMEM((PARTS, height, block), f32),
            pltpu.VMEM((n_col, height, block), bf16),
            pltpu.VMEM((n_row, height, block), bf16),
            pltpu.VMEM((2, PARTS, n_col, height, block), bf16),
            pltpu.VMEM((2, PARTS, n_row, height, block), bf16),
            pltpu.VMEM((slots + 1, height, block), f32),
            pltpu.VMEM((slots + 1, height, block), f32),
            pltpu.VMEM((2, PARTS, chips, height, block), f32),
            pltpu.VMEM((2, PARTS, chips, height, block), f32),
        ]
        + [pltpu.VMEM((2, PARTS, chips, height, block), i16)] * 4
        + [
            pltpu.SMEM((n_col,), jnp.int32),
            pltpu.SMEM((n_col,), jnp.int32),
            pltpu.SMEM((slots,), jnp.int32),
            pltpu.SMEM((chips,), jnp.int32),
            pltpu.SMEM((chips,), jnp.int32),
            pltpu.SMEM((chips,), jnp.int32),
            pltpu.SMEM((n_col,), jnp.int32),
            pltpu.SMEM((slots,), jnp.int32),
            pltpu.SMEM((slots,), jnp.int32),
            dma((4,)),
        ]
        + [dma((2, PARTS, n_col))] * 8
        + [dma((2, PARTS, chips // BATCH))] * 2
        + [dma((2, PARTS, 2))] * 2,
        compiler_params=pltpu.CompilerParams(
            collective_id=0, has_side_effects=True, vmem_limit_bytes=60 * 1024 * 1024
        ),
        cost_estimate=pl.CostEstimate(
            flops=8 * slots * count * block * block, bytes_accessed=2 * slots * block * block, transcendentals=0
        ),
    )(tile_row[0], tile_col[0], vectors, tiles[0, 0])


def solution(mesh):
    placed = (
        P(None, ("row", "col")),
        P("row", "col", None, None, None),
        P("row", "col", None),
        P("row", "col", None),
    )
    return jax.shard_map(
        shards,
        mesh=mesh,
        in_specs=placed,
        out_specs=(P(None, ("row", "col")), P(None, ("row", "col"))),
        check_vma=False,
    )
```
